32 devices in a mesh: grp: 4 (over x, core), dev: 8 (over z, y).
Axes of the slice: x: 2, y: 2, z: 4, core: 2. Of those that a mesh axis runs over, the one named last changes fastest.
Arguments:
- queries: bfloat16 [8192, 768], P(('grp', 'dev')), may hold values from -1.796875 to 1.796875
- query_slots: int32 [8192], P('grp'), may hold values from 0 to 2047, as said below
- w_res: bfloat16 [768, 768], replicated, may hold values from -0.21875 to 0.21875
- labels: bfloat16 [640, 128, 768], P(('grp', 'dev')), may hold values from -0.71875 to 0.71875
- blocks: int32 [64, 12], P('grp'), may hold values from 0 to 639, as said below
- positives: int32 [8192, 4], P(('grp', 'dev')), may hold values from 0 to 81919, as said below
Outputs:
- query_loss: float32 [8192], P(('grp', 'dev'))
- query_grad: bfloat16 [8192, 768], P(('grp', 'dev'))
- label_grad: bfloat16 [640, 128, 768], P(('grp', 'dev'))
- residual_grad: bfloat16 [768, 768], replicated
The draws below stay inside these ranges and needn't reach their ends.
Inputs may be any that keep to these rules, and one draw needn't show every extreme that they name: `query_slots`: the rows of one grp index (rows g * 256 * 8 onward) hold a permutation of 0 to 2047; a place // 256 is the dev index that owns the query's cluster, and the 256 rows of every device send exactly 32 queries to each owner. Row c lists 12 different blocks, all held by devices of the same grp index as the cluster's owner (device c // 2). The 2 clusters of one device list at most 16 distinct blocks, of which at most 2 are held by any one device; for every device's clusters some holder reaches 2. `positives`: the 4 labels of row r are different and lie in 4 different blocks listed for cluster r // 128.
All inputs are finite; a program needn't handle non-finite values.
Results may differ from the reference program's by a relative error of at most 0.0047.
The reference program's roundings to bfloat16 on the way (of `hidden`, `clustered`, `errors`, `cluster_grad`, `partial`, `hidden_grad` and `pre_grad`) count: a program that leaves them out, or rounds other values in their place, can miss the bound.
Values may be sent and summed in bfloat16 or wider, within the bound.
A program may use at most 128 MiB of HBM per device.

```python
from functools import partial
import jax
import jax.numpy as jnp
from jax import lax

D = 768
BLK = 128
CSIZE = 128
SHORT = 12
NPOS = 4
POOL = 16
BLK_DEV = 20
CL_DEV = 2
Q_DEV = 256
CAPU = 2
QUERIES = 8192
CLUSTERS = 64
NBLK = 640
N_GRP = 4
N_DEV = 8
DEVICES = 32


def pool_lists(key):

    def one_device(device_key, device):
        owner_key, base_key, pick_key = jax.random.split(device_key, 3)
        spread = jnp.repeat(jnp.arange(N_DEV, dtype=jnp.int32), CAPU)
        owners = jax.random.permutation(owner_key, spread)[:POOL]
        positions = jnp.arange(POOL, dtype=jnp.int32)
        earlier = positions[None, :] < positions[:, None]
        ranking = jnp.sum((owners[:, None] == owners[None, :]) & earlier, axis=1).astype(jnp.int32)
        starts = jax.random.randint(base_key, (N_DEV,), 0, BLK_DEV, dtype=jnp.int32)
        within = (starts[owners] + ranking) % BLK_DEV
        group_number = device // N_DEV
        pool_ids = (group_number * N_DEV + owners) * BLK_DEV + within
        counts = jnp.sum(owners[:, None] == jnp.arange(N_DEV, dtype=jnp.int32)[None, :], axis=0)
        busiest = jnp.argmax(counts).astype(jnp.int32)
        forced = (owners == busiest).astype(jnp.int32)

        def one_cluster(cluster_key):
            score_key, order_key = jax.random.split(cluster_key)
            scores = jax.random.permutation(score_key, POOL).astype(jnp.int32) - POOL * forced
            picked = jnp.argsort(scores)[:SHORT]
            return jax.random.permutation(order_key, pool_ids[picked])
        return jax.vmap(one_cluster)(jax.random.split(pick_key, CL_DEV))
    devices_all = jnp.arange(DEVICES, dtype=jnp.int32)
    device_keys = jax.vmap(partial(jax.random.fold_in, key))(devices_all)
    return jax.vmap(one_device)(device_keys, devices_all).reshape(CLUSTERS, SHORT).astype(jnp.int32)


def draw_blocks(key, part):
    return pool_lists(jax.random.fold_in(key, 7))


def draw_positives(key, part):
    lists = pool_lists(jax.random.fold_in(key, 7))
    start_key, label_key = jax.random.split(jax.random.fold_in(key, 11))
    cluster_of = jnp.arange(QUERIES, dtype=jnp.int32) // CSIZE
    starts = jax.random.randint(start_key, (QUERIES,), 0, SHORT, dtype=jnp.int32)
    columns = (starts[:, None] + jnp.arange(NPOS, dtype=jnp.int32)[None, :]) % SHORT
    inside = jax.random.randint(label_key, (QUERIES, NPOS), 0, BLK, dtype=jnp.int32)
    return (lists[cluster_of[:, None], columns] * BLK + inside).astype(jnp.int32)


def draw_query_slots(key, part):
    per_peer = Q_DEV // N_DEV
    group_rows = Q_DEV * N_DEV

    def one_group(group_key):
        dest_key, place_key = jax.random.split(group_key)
        base_row = jnp.repeat(jnp.arange(N_DEV, dtype=jnp.int32), per_peer)
        dest_keys = jax.random.split(dest_key, N_DEV)
        targets = jax.vmap(jax.random.permutation, (0, None))(dest_keys, base_row).reshape(group_rows)
        sort_keys = targets * group_rows + jnp.arange(group_rows, dtype=jnp.int32)
        order = jnp.argsort(sort_keys)
        place_keys = jax.random.split(place_key, N_DEV)
        shuffles = jax.vmap(jax.random.permutation, (0, None))(place_keys, jnp.arange(Q_DEV, dtype=jnp.int32))
        sorted_owner = jnp.arange(group_rows, dtype=jnp.int32) // Q_DEV
        sorted_slots = sorted_owner * Q_DEV + shuffles.reshape(group_rows)
        return jnp.zeros((group_rows,), jnp.int32).at[order].set(sorted_slots.astype(jnp.int32))
    group_keys = jax.random.split(key, DEVICES // N_DEV)
    return jax.vmap(one_group)(group_keys).reshape(QUERIES).astype(jnp.int32)


def shard_levels(rng, dims, shards, smallest, high):
    loudness, own = 1.0, jax.random.fold_in(rng, 6)
    for axis_at, shards_of in shards:
        heights = jnp.exp(jax.random.uniform(jax.random.fold_in(own, axis_at), (shards_of,), jnp.float32, smallest / len(shards), high / len(shards)))
        loudness = loudness * jnp.repeat(heights, dims[axis_at] // shards_of).reshape([-1 if axis == axis_at else 1 for axis in range(len(dims))])
    return loudness


def scatter_about(stream_key, extent, deviation, most, cuts=(), kind=jnp.bfloat16):
    values = jax.random.normal(stream_key, extent, jnp.float32) * deviation
    if len(cuts) > 0:
        values = shard_levels(stream_key, extent, cuts, -0.22, 0.18) * values
    return jnp.clip(values, min=-most, max=most).astype(kind)


def setup_inputs(seed: int = 0) -> dict:
    streams_of = jax.random.split(jax.random.key(seed), 7)
    return {
        "queries": scatter_about(streams_of[0], (QUERIES, D), 0.3, 1.796875, ((0, 32),)),
        "query_slots": draw_query_slots(jax.random.fold_in(streams_of[6], 71), 0),
        "w_res": scatter_about(streams_of[2], (D, D), D ** -0.5, 0.21875),
        "labels": scatter_about(streams_of[3], (NBLK, BLK, D), 0.12, 0.71875, ((0, 32),)),
        "blocks": draw_blocks(jax.random.fold_in(streams_of[6], 71), 0),
        "positives": draw_positives(jax.random.fold_in(streams_of[6], 71), 0),
    }


def activate(values):
    return jax.nn.gelu(values, approximate=True)

def activate_slope(values):
    return jax.vjp(activate, values)[1](jnp.ones_like(values))[0]

def reference(queries, query_slots, w_res, labels, blocks, positives):
    group_rows = Q_DEV * N_DEV
    group_clusters = CL_DEV * N_DEV
    group_blocks = BLK_DEV * N_DEV
    offsets = jnp.arange(BLK, dtype=jnp.int32)

    def group_step(weight_total, inputs):
        group_number, group_input, places, lists, wanted, group_labels = inputs
        pre = jnp.dot(group_input, w_res, preferred_element_type=jnp.float32)
        hidden = (group_input.astype(jnp.float32) + activate(pre)).astype(jnp.bfloat16)
        clustered = jnp.zeros_like(hidden).at[places].set(hidden)
        block_base = group_number * group_blocks

        def device_step(totals, pieces):
            cluster_rows, cluster_ids, cluster_pos = pieces
            local_ids = (cluster_ids - block_base).astype(jnp.int32)
            chosen = group_labels[local_ids]
            rows_wide = cluster_rows.astype(jnp.float32)
            chosen_wide = chosen.astype(jnp.float32)
            logits = jnp.einsum('cqd,ckjd->cqkj', rows_wide, chosen_wide, precision=lax.Precision.HIGHEST)
            label_ids = cluster_ids[:, :, None] * BLK + offsets[None, None, :]
            hits = label_ids[:, None, :, :, None] == cluster_pos[:, :, None, None, :]
            targets = jnp.any(hits, axis=-1).astype(jnp.float32)
            loss_rows = lax.optimization_barrier(jnp.mean(jax.nn.softplus(logits) - targets * logits, axis=(2, 3)))
            errors = (jax.nn.sigmoid(logits) - targets).astype(jnp.bfloat16)
            errors_wide = errors.astype(jnp.float32)
            grad_rows = jnp.einsum('cqkj,ckjd->cqd', errors_wide, chosen_wide, precision=lax.Precision.HIGHEST).astype(jnp.bfloat16)
            terms = jnp.einsum('cqkj,cqd->ckjd', errors_wide, rows_wide, precision=lax.Precision.HIGHEST)
            terms = terms.reshape(-1, BLK, D)
            flat_ids = local_ids.reshape(-1)
            same_block = flat_ids[:, None] == flat_ids[None, :]
            first_seen = jnp.argmax(same_block, axis=1).astype(jnp.int32)
            summed = jax.ops.segment_sum(terms, first_seen, num_segments=flat_ids.shape[0])
            rounded = lax.optimization_barrier(summed.astype(jnp.bfloat16)).astype(jnp.float32)
            totals = totals.at[flat_ids].add(rounded)
            return (totals, (loss_rows, grad_rows))
        start = jnp.zeros((group_blocks, BLK, D), jnp.float32)
        pieces = (clustered.reshape(N_DEV, CL_DEV, CSIZE, D), lists.reshape(N_DEV, CL_DEV, SHORT), wanted.reshape(N_DEV, CL_DEV, CSIZE, NPOS))
        totals, (loss_rows, grad_rows) = lax.scan(device_step, start, pieces)
        cluster_grad = grad_rows.reshape(group_rows, D)
        hidden_grad = cluster_grad[places]
        pre_grad = (hidden_grad.astype(jnp.float32) * activate_slope(pre)).astype(jnp.bfloat16)
        back_term = jnp.dot(pre_grad, w_res.T, preferred_element_type=jnp.float32)
        query_grad = (hidden_grad.astype(jnp.float32) + back_term).astype(jnp.bfloat16)
        weight_total = weight_total + jnp.dot(group_input.T, pre_grad, preferred_element_type=jnp.float32)
        return (weight_total, (loss_rows.reshape(group_rows), query_grad, totals.astype(jnp.bfloat16)))
    inputs = (jnp.arange(N_GRP, dtype=jnp.int32), queries.reshape(N_GRP, group_rows, D), query_slots.reshape(N_GRP, group_rows), blocks.reshape(N_GRP, group_clusters, SHORT), positives.reshape(N_GRP, group_rows, NPOS), labels.reshape(N_GRP, group_blocks, BLK, D))
    weight_total, (loss_rows, query_grad, label_grad) = lax.scan(group_step, jnp.zeros((D, D), jnp.float32), inputs)
    residual_grad = (weight_total * QUERIES ** (-0.5)).astype(jnp.bfloat16)
    return (loss_rows.reshape(QUERIES), query_grad.reshape(QUERIES, D), label_grad.reshape(NBLK, BLK, D), residual_grad)
```

```python
import functools

import jax
import jax.numpy as jnp
from jax import lax
from jax.experimental import pallas as pl
from jax.experimental.pallas import tpu as pltpu
from jax.sharding import PartitionSpec as P

BLK = 128
CSIZE = 128
SHORT = 12
NPOS = 4
UNITS = 2
MESH = pl.DeviceIdType.MESH
F32 = jnp.float32
BF16 = jnp.bfloat16


def activate(values):
    return jax.nn.gelu(values, approximate=True)


def activate_slope(values):
    return jax.vjp(activate, values)[1](jnp.ones_like(values))[0]


def remote(src, dst, send, recv, where):
    return pltpu.make_async_remote_copy(
        src_ref=src, dst_ref=dst, send_sem=send, recv_sem=recv, device_id=where, device_id_type=MESH
    )


def greet(targets):
    barrier = pltpu.get_barrier_semaphore()
    for where in targets:
        pl.semaphore_signal(barrier, inc=1, device_id=where, device_id_type=MESH)
    pl.semaphore_wait(barrier, len(targets))


def dev_peers(peers):
    me = lax.axis_index("dev")
    return [{"dev": lax.rem(me + d, peers)} for d in range(1, peers)]


def gather_kernel(peers, hid, meta, hall, mall, own, zs, zr, ys, yr, ms, mr):
    me = lax.axis_index("dev")
    inner, outer, lines = lax.rem(me, 2), me // 2, peers // 2
    partner = {"dev": outer * 2 + 1 - inner}
    greet(dev_peers(peers))
    local_h = pltpu.make_async_copy(hid, hall.at[me], own.at[0])
    local_m = pltpu.make_async_copy(meta, mall.at[me], own.at[1])
    along, across, small = [], [], []
    across.append(remote(hid, hall.at[me], ys.at[0], yr.at[0], partner))
    for d in range(1, lines):
        there = {"dev": lax.rem(outer + d, lines) * 2 + inner}
        along.append(remote(hid, hall.at[me], zs.at[d], zr.at[d], there))
    for d in range(1, peers):
        there = {"dev": lax.rem(me + d, peers)}
        small.append(remote(meta, mall.at[me], ms.at[d], mr.at[d], there))
    for copy in along + across + small:
        copy.start()
    local_h.start()
    local_m.start()
    for d in range(1, lines):
        source = lax.rem(outer + lines - d, lines) * 2 + inner
        along[d - 1].wait_recv()
        copy = remote(hall.at[source], hall.at[source], ys.at[d], yr.at[d], partner)
        copy.start()
        across.append(copy)
    for copy in along:
        copy.wait_send()
    for copy in across + small:
        copy.wait()
    local_h.wait()
    local_m.wait()


def cluster_kernel(table, hall, meta, labels, grads, losses, label_grad, total):
    step = pl.program_id(0)
    peers, _, per, width = hall.shape
    rows = peers * per

    @pl.when(step == 0)
    def _():
        total[...] = jnp.zeros_like(total)

    data = hall[...].reshape(rows, width)
    member = meta[0, NPOS:NPOS + 1, :]
    lanes = lax.broadcasted_iota(jnp.int32, (BLK, rows), 0)
    grad = jnp.zeros((rows, width), F32)
    loss = jnp.zeros((1, rows), F32)
    for unit in range(UNITS):
        block = table[step, unit]
        base = table[step, 6] + block * BLK
        listed = jnp.where(member == 0, table[step, 2 + 2 * unit], table[step, 3 + 2 * unit])
        live = listed > 0
        vectors = labels[block]
        logits = lax.dot_general(
            vectors, data, (((1,), (1,)), ((), ())), preferred_element_type=F32
        )
        hit = lanes == meta[0, 0:1, :] - base
        for n in range(1, NPOS):
            hit = hit | (lanes == meta[0, n:n + 1, :] - base)
        small = jnp.exp(-jnp.abs(logits))
        soft = jnp.maximum(logits, 0.0) + jnp.log1p(small)
        loss = loss + jnp.where(
            live, jnp.sum(soft - jnp.where(hit, logits, 0.0), axis=0, keepdims=True), 0.0
        )
        chance = jnp.where(logits >= 0, 1.0, small) / (1.0 + small)
        wrong = jnp.where(live, chance - jnp.where(hit, 1.0, 0.0), 0.0).astype(BF16)
        grad = grad + lax.dot_general(
            wrong, vectors, (((0,), (0,)), ((), ())), preferred_element_type=F32
        )
        term = jnp.dot(wrong, data, preferred_element_type=F32)
        total[block] = total[block] + term.astype(BF16).astype(F32)
    grads[...] = grad.astype(BF16).reshape(grads.shape)
    losses[0] = jnp.broadcast_to(loss * (1.0 / (SHORT * BLK)), losses.shape[1:])

    @pl.when(step == pl.num_programs(0) - 1)
    def _():
        label_grad[...] = total[...].astype(BF16)


def scatter_kernel(peers, grads, losses, out, loss_out, yb, hb, zb, lb, ys, yr, zs, zr, ls, lr):
    me = lax.axis_index("dev")
    inner, outer, lines = lax.rem(me, 2), me // 2, peers // 2
    partner = {"dev": outer * 2 + 1 - inner}
    greet(dev_peers(peers))
    across, along, small = [], [], []
    for k in range(lines):
        line = lax.rem(outer + 1 + k, lines)
        across.append(remote(grads.at[line * 2 + 1 - inner], yb.at[k], ys.at[k], yr.at[k], partner))
    for d in range(1, peers):
        dest = lax.rem(me + d, peers)
        small.append(remote(losses.at[dest], lb.at[d], ls.at[d], lr.at[d], {"dev": dest}))
    for copy in across + small:
        copy.start()
    for k in range(lines):
        line = lax.rem(outer + 1 + k, lines)
        across[k].wait_recv()
        pair = grads[line * 2 + inner].astype(F32) + yb[k].astype(F32)
        hb[k] = pair.astype(BF16)
        if k < lines - 1:
            copy = remote(hb.at[k], zb.at[k], zs.at[k], zr.at[k], {"dev": line * 2 + inner})
            copy.start()
            along.append(copy)
    for copy in small:
        copy.wait()
    loss = losses[me]
    for d in range(1, peers):
        loss = loss + lb[d]
    loss_out[...] = loss
    for copy in along:
        copy.wait()
    acc = hb[lines - 1].astype(F32)
    for k in range(lines - 1):
        acc = acc + zb[k].astype(F32)
    out[...] = acc.astype(BF16)
    for copy in across:
        copy.wait_send()


def sum_kernel(peers, groups, scale, term, out, b1, t1, b2, t2, b3, sends, recvs):
    me, group = lax.axis_index("dev"), lax.axis_index("grp")
    core, chip, chips = lax.rem(group, 2), group // 2, groups // 2
    partner = {"grp": chip * 2 + 1 - core}
    chip_at = [lax.rem(chip + d, chips) for d in range(chips)]
    dev_at = [lax.rem(me + d, peers) for d in range(peers)]
    greet(
        [partner]
        + [{"grp": chip_at[d] * 2 + core} for d in range(1, chips)]
        + [{"dev": dev_at[d]} for d in range(1, peers)]
    )
    used = [0]

    def make(src, dst, where):
        at = used[0]
        used[0] += 1
        return remote(src, dst, sends.at[at], recvs.at[at], where)

    def run(copies):
        for copy in copies:
            copy.start()
        for copy in copies:
            copy.wait()

    run([make(term.at[1 - core], b1, partner)])
    t1[...] = (term[core].astype(F32) + b1[...].astype(F32)).astype(BF16)
    run([make(t1.at[chip_at[d]], b2.at[d], {"grp": chip_at[d] * 2 + core}) for d in range(1, chips)])
    acc = t1[chip].astype(F32)
    for d in range(1, chips):
        acc = acc + b2[d].astype(F32)
    t2[...] = acc.astype(BF16)
    run([make(t2.at[dev_at[d]], b3.at[d], {"dev": dev_at[d]}) for d in range(1, peers)])
    acc = t2[me].astype(F32)
    for d in range(1, peers):
        acc = acc + b3[d].astype(F32)
    out[core, chip, me] = (acc * scale).astype(BF16)
    mine = out.at[core, chip, me]
    run([make(mine, mine, {"dev": dev_at[d]}) for d in range(1, peers)])
    mine = out.at[core, chip]
    run([make(mine, mine, {"grp": chip_at[d] * 2 + core}) for d in range(1, chips)])
    run([make(out.at[core], out.at[core], partner)])


def params(collective=None):
    more = {} if collective is None else dict(collective_id=collective, has_side_effects=True)
    return pltpu.CompilerParams(vmem_limit_bytes=48 * 1024 * 1024, **more)


def local(queries, query_slots, w_res, labels, blocks, positives):
    peers = lax.axis_size("dev")
    groups = lax.axis_size("grp")
    me = lax.axis_index("dev")
    group = lax.axis_index("grp")
    rows, width = queries.shape
    held = labels.shape[0]
    per = rows // peers
    lines = peers // 2
    chips = groups // 2
    vmem = pl.BlockSpec(memory_space=pltpu.VMEM)
    anywhere = pl.BlockSpec(memory_space=pl.ANY)
    dma = pltpu.SemaphoreType.DMA

    slot_grid = query_slots.reshape(peers, rows)
    slot_sorted = jnp.sort(slot_grid, axis=1)
    own_slots = lax.dynamic_index_in_dim(slot_grid, me, 0, keepdims=False)
    own_sorted = lax.dynamic_index_in_dim(slot_sorted, me, 0, keepdims=False)
    order = (own_sorted[:, None] == own_slots[None, :]).astype(BF16)
    place = lax.dynamic_slice_in_dim(slot_sorted, me * per, per, 1).reshape(rows) - me * rows
    arrange = place[None, :] == jnp.arange(rows, dtype=jnp.int32)[:, None]
    wanted = jnp.sum(jnp.where(arrange[None], positives.T[:, :, None], 0), axis=1)
    meta = jnp.concatenate(
        [wanted, (place // CSIZE)[None], jnp.zeros((8 - NPOS - 1, rows), jnp.int32)], axis=0
    )
    first = (group * peers + me) * held
    listed = blocks.reshape(peers, rows // CSIZE, SHORT) - first
    inside = (listed >= 0) & (listed < held)
    low = jnp.min(jnp.where(inside, listed, held), axis=(1, 2))
    high = jnp.max(jnp.where(inside, listed, -1), axis=(1, 2))
    flag_low = jnp.any(inside & (listed == low[:, None, None]), axis=2).astype(jnp.int32)
    flag_high = jnp.any(inside & (listed == high[:, None, None]), axis=2).astype(jnp.int32)
    flag_high = jnp.where((high > low)[:, None], flag_high, 0)
    table = jnp.concatenate(
        [
            jnp.minimum(low, held - 1)[:, None],
            jnp.maximum(high, 0)[:, None],
            flag_low,
            flag_high,
            jnp.broadcast_to(first * BLK, (peers, 1)),
        ],
        axis=1,
    )

    ordered = jnp.dot(order, queries, preferred_element_type=F32).astype(BF16)
    pre = jnp.dot(ordered, w_res, preferred_element_type=F32)
    hidden = (ordered.astype(F32) + activate(pre)).astype(BF16)

    hall, mall = pl.pallas_call(
        functools.partial(gather_kernel, peers),
        out_shape=(
            jax.ShapeDtypeStruct((peers, peers, per, width), BF16),
            jax.ShapeDtypeStruct((peers, 8, rows), jnp.int32),
        ),
        in_specs=[anywhere, anywhere],
        out_specs=(anywhere, anywhere),
        scratch_shapes=[
            dma((2,)), dma((lines,)), dma((lines,)), dma((lines,)), dma((lines,)),
            dma((peers,)), dma((peers,)),
        ],
        compiler_params=params(0),
    )(hidden.reshape(peers, per, width), meta)

    grads, losses, label_grad = pl.pallas_call(
        cluster_kernel,
        grid_spec=pltpu.PrefetchScalarGridSpec(
            num_scalar_prefetch=1,
            grid=(peers,),
            in_specs=[
                pl.BlockSpec((peers, 1, per, width), lambda p, t: (0, p, 0, 0)),
                pl.BlockSpec((1, 8, rows), lambda p, t: (p, 0, 0)),
                pl.BlockSpec((held, BLK, width), lambda p, t: (0, 0, 0)),
            ],
            out_specs=[
                pl.BlockSpec((peers, 1, per, width), lambda p, t: (0, p, 0, 0)),
                pl.BlockSpec((1, 8, rows), lambda p, t: (p, 0, 0)),
                pl.BlockSpec((held, BLK, width), lambda p, t: (0, 0, 0)),
            ],
            scratch_shapes=[pltpu.VMEM((held, BLK, width), F32)],
        ),
        out_shape=(
            jax.ShapeDtypeStruct((peers, peers, per, width), BF16),
            jax.ShapeDtypeStruct((peers, 8, rows), F32),
            jax.ShapeDtypeStruct(labels.shape, BF16),
        ),
        compiler_params=params(),
    )(table, hall, mall, labels)

    hidden_grad, loss_sum = pl.pallas_call(
        functools.partial(scatter_kernel, peers),
        out_shape=(
            jax.ShapeDtypeStruct((peers, per, width), BF16),
            jax.ShapeDtypeStruct((8, rows), F32),
        ),
        in_specs=[vmem, vmem],
        out_specs=(vmem, vmem),
        scratch_shapes=[
            pltpu.VMEM((lines, peers, per, width), BF16),
            pltpu.VMEM((lines, peers, per, width), BF16),
            pltpu.VMEM((lines, peers, per, width), BF16),
            pltpu.VMEM((peers, 8, rows), F32),
            dma((lines,)), dma((lines,)), dma((lines,)), dma((lines,)),
            dma((peers,)), dma((peers,)),
        ],
        compiler_params=params(1),
    )(grads, losses)
    hidden_grad = hidden_grad.reshape(rows, width).astype(F32)

    loss_rows = jnp.sum(jnp.where(arrange, loss_sum[0][None, :], 0.0), axis=1)
    grad_pre = (hidden_grad * activate_slope(pre)).astype(BF16)
    weight_term = lax.dot_general(
        ordered, grad_pre, (((0,), (0,)), ((), ())), preferred_element_type=F32
    )
    tall, wide = width // (2 * chips * lines), width // 2
    pieces = weight_term.astype(BF16).reshape(2, chips, lines, tall, 2, wide)
    pieces = pieces.transpose(0, 1, 4, 2, 3, 5).reshape(2, chips, peers, tall, wide)
    count = 2 + 2 * (chips - 1) + 2 * (peers - 1)
    summed = pl.pallas_call(
        functools.partial(
            sum_kernel, peers, groups, float(rows * peers * groups) ** (-0.5)
        ),
        out_shape=jax.ShapeDtypeStruct(pieces.shape, BF16),
        in_specs=[vmem],
        out_specs=vmem,
        scratch_shapes=[
            pltpu.VMEM((chips, peers, tall, wide), BF16),
            pltpu.VMEM((chips, peers, tall, wide), BF16),
            pltpu.VMEM((chips, peers, tall, wide), BF16),
            pltpu.VMEM((peers, tall, wide), BF16),
            pltpu.VMEM((peers, tall, wide), BF16),
            dma((count,)), dma((count,)),
        ],
        compiler_params=params(2),
    )(pieces)
    residual_grad = summed.reshape(2, chips, 2, lines, tall, wide)
    residual_grad = residual_grad.transpose(0, 1, 3, 4, 2, 5).reshape(width, width)

    back_term = jnp.einsum("qe,de->qd", grad_pre, w_res, preferred_element_type=F32)
    query_grad = (hidden_grad + back_term).astype(BF16)
    query_grad = lax.dot_general(
        order, query_grad, (((0,), (0,)), ((), ())), preferred_element_type=F32
    ).astype(BF16)
    return loss_rows, query_grad, label_grad, residual_grad


def solution(mesh):
    in_specs = (
        P(("grp", "dev"), None),
        P("grp"),
        P(),
        P(("grp", "dev"), None, None),
        P("grp", None),
        P(("grp", "dev"), None),
    )
    out_specs = (P(("grp", "dev")), P(("grp", "dev"), None), P(("grp", "dev"), None, None), P())
    return jax.shard_map(local, mesh=mesh, in_specs=in_specs, out_specs=out_specs, check_vma=False)
```

```python
import functools

import jax
import jax.numpy as jnp
from jax import lax
from jax.experimental import pallas as pl
from jax.experimental.pallas import tpu as pltpu
from jax.sharding import PartitionSpec as P

BLK = 128
CSIZE = 128
SHORT = 12
NPOS = 4
UNITS = 2
MESH = pl.DeviceIdType.MESH
F32 = jnp.float32
BF16 = jnp.bfloat16


def activate(values):
    return jax.nn.gelu(values, approximate=True)


def activate_slope(values):
    return jax.vjp(activate, values)[1](jnp.ones_like(values))[0]


def remote(src, dst, send, recv, where):
    return pltpu.make_async_remote_copy(
        src_ref=src, dst_ref=dst, send_sem=send, recv_sem=recv, device_id=where, device_id_type=MESH
    )


def greet(targets):
    barrier = pltpu.get_barrier_semaphore()
    for where in targets:
        pl.semaphore_signal(barrier, inc=1, device_id=where, device_id_type=MESH)
    pl.semaphore_wait(barrier, len(targets))


def dev_peers(peers):
    me = lax.axis_index("dev")
    return [{"dev": lax.rem(me + d, peers)} for d in range(1, peers)]


def gather_kernel(peers, hid, meta, hall, mall, own, us, ur, ds, dr, ys, yr, ms, mr):
    me = lax.axis_index("dev")
    inner, outer, lines = lax.rem(me, 2), me // 2, peers // 2
    top = lines - 1
    partner = {"dev": outer * 2 + 1 - inner}
    above, below = {"dev": me + 2}, {"dev": me - 2}
    greet(dev_peers(peers))

    def up(k, held=None):
        spot = hall.at[me - 2 * k]
        return remote(spot if held is None else held, spot, us.at[k], ur.at[k], above)

    def down(k, held=None):
        spot = hall.at[me + 2 * k]
        return remote(spot if held is None else held, spot, ds.at[k], dr.at[k], below)

    def across(line, held=None):
        spot = hall.at[line * 2 + inner]
        return remote(spot if held is None else held, spot, ys.at[line], yr.at[line], partner)

    @pl.when(outer < top)
    def _():
        up(0, hid).start()

    @pl.when(outer > 0)
    def _():
        down(0, hid).start()

    across(outer, hid).start()
    local_h = pltpu.make_async_copy(hid, hall.at[me], own.at[0])
    local_m = pltpu.make_async_copy(meta, mall.at[me], own.at[1])
    local_h.start()
    local_m.start()
    small = []
    for d in range(1, peers):
        there = {"dev": lax.rem(me + d, peers)}
        small.append(remote(meta, mall.at[me], ms.at[d], mr.at[d], there))
    for copy in small:
        copy.start()
    for k in range(lines - 1):

        @pl.when(outer >= k + 1)
        def _():
            spot = hall.at[me - 2 * (k + 1)]
            remote(spot, spot, us.at[k], ur.at[k], below).wait_recv()

            @pl.when(outer < top)
            def _():
                up(k + 1).start()

            across(outer - 1 - k).start()

        @pl.when(outer + k + 1 <= top)
        def _():
            spot = hall.at[me + 2 * (k + 1)]
            remote(spot, spot, ds.at[k], dr.at[k], above).wait_recv()

            @pl.when(outer > 0)
            def _():
                down(k + 1).start()

            across(outer + 1 + k).start()

    for k in range(lines):

        @pl.when((outer >= k) & (outer < top))
        def _():
            up(k).wait_send()

        @pl.when((outer + k <= top) & (outer > 0))
        def _():
            down(k).wait_send()

    for line in range(lines):
        across(line).wait()
    for copy in small:
        copy.wait()
    local_h.wait()
    local_m.wait()


def cluster_kernel(table, hall, meta, labels, grads, losses, label_grad, total):
    step = pl.program_id(0)
    peers, owners, per, width = hall.shape
    rows = peers * per

    @pl.when(step == 0)
    def _():
        total[...] = jnp.zeros_like(total)

    lanes = lax.broadcasted_iota(jnp.int32, (BLK, rows), 0)
    for owner in range(owners):
        at = step * owners + owner
        data = hall[:, owner].reshape(rows, width)
        member = meta[owner, NPOS:NPOS + 1, :]
        vectors = jnp.concatenate([labels[table[at, unit]] for unit in range(UNITS)], axis=0)
        logits = lax.dot_general(
            vectors, data, (((1,), (1,)), ((), ())), preferred_element_type=F32
        )
        small = jnp.exp(-jnp.abs(logits))
        soft = jnp.maximum(logits, 0.0) + jnp.log1p(small)
        chance = jnp.where(logits >= 0, 1.0, small) / (1.0 + small)
        loss = jnp.zeros((1, rows), F32)
        parts = []
        for unit in range(UNITS):
            base = table[at, 6] + table[at, unit] * BLK
            listed = jnp.where(member == 0, table[at, 2 + 2 * unit], table[at, 3 + 2 * unit])
            live = listed > 0
            span = slice(unit * BLK, (unit + 1) * BLK)
            hit = lanes == meta[owner, 0:1, :] - base
            for n in range(1, NPOS):
                hit = hit | (lanes == meta[owner, n:n + 1, :] - base)
            gap = soft[span] - jnp.where(hit, logits[span], 0.0)
            loss = loss + jnp.where(live, jnp.sum(gap, axis=0, keepdims=True), 0.0)
            parts.append(jnp.where(live, chance[span] - jnp.where(hit, 1.0, 0.0), 0.0))
        wrong = jnp.concatenate(parts, axis=0).astype(BF16)
        grad = lax.dot_general(
            wrong, vectors, (((0,), (0,)), ((), ())), preferred_element_type=F32
        )
        term = jnp.dot(wrong, data, preferred_element_type=F32).astype(BF16).astype(F32)
        for unit in range(UNITS):
            block = table[at, unit]
            total[block] = total[block] + term[unit * BLK:(unit + 1) * BLK]
        grads[:, owner] = grad.astype(BF16).reshape(peers, per, width)
        losses[owner] = jnp.broadcast_to(loss * (1.0 / (SHORT * BLK)), losses.shape[1:])

    @pl.when(step == pl.num_programs(0) - 1)
    def _():
        label_grad[...] = total[...].astype(BF16)


def scatter_kernel(
    peers, grads, losses, out, loss_out, yb, hb, rb, acc, lb, ys, yr, zs, zr, ls, lr
):
    me = lax.axis_index("dev")
    inner, outer, lines = lax.rem(me, 2), me // 2, peers // 2
    top = lines - 1
    partner = {"dev": outer * 2 + 1 - inner}
    orders = [sorted(range(lines), key=lambda at: -abs(at - o)) for o in range(lines)]
    greet(dev_peers(peers))

    def pick(k):
        line = orders[0][k]
        for o in range(1, lines):
            line = jnp.where(outer == o, orders[o][k], line)
        return line

    picked = [pick(k) for k in range(lines - 1)] + [outer]
    across, along, small = [], [], []
    for k, line in enumerate(picked):
        across.append(remote(grads.at[line * 2 + 1 - inner], yb.at[k], ys.at[k], yr.at[k], partner))
    for d in range(1, peers):
        dest = lax.rem(me + d, peers)
        small.append(remote(losses.at[dest], lb.at[d], ls.at[d], lr.at[d], {"dev": dest}))
    for copy in across + small:
        copy.start()

    def pair(k):
        return grads[picked[k] * 2 + inner].astype(F32) + yb[k].astype(F32)

    for k in range(lines - 1):
        line = picked[k]
        way = jnp.where(line > outer, 0, 1)
        ahead = me + 2 - 4 * way
        feeds = jnp.where(line > outer, outer, top - outer)
        copy = remote(hb.at[k], rb.at[way, line], zs.at[k], zr.at[way, line], {"dev": ahead})
        across[k].wait_recv()

        @pl.when(feeds == 0)
        def _():
            hb[k] = pair(k).astype(BF16)

        @pl.when(feeds > 0)
        def _():
            copy.wait_recv()
            hb[k] = (pair(k) + rb[way, line].astype(F32)).astype(BF16)

        copy.start()
        along.append(copy)
    for copy in small:
        copy.wait()
    loss = losses[me]
    for d in range(1, peers):
        loss = loss + lb[d]
    loss_out[...] = loss
    across[top].wait_recv()
    acc[...] = pair(top)
    for way, present in enumerate((outer > 0, outer < top)):

        @pl.when(present)
        def _():
            spot = rb.at[way, outer]
            near = {"dev": me - 2 + 4 * way}
            remote(spot, spot, zs.at[0], zr.at[way, outer], near).wait_recv()
            acc[...] += rb[way, outer].astype(F32)

    out[...] = acc[...].astype(BF16)
    for copy in across + along:
        copy.wait_send()


def sum_kernel(peers, groups, scale, term, out, b1, t1, b2, t2, b3, sends, recvs):
    me, group = lax.axis_index("dev"), lax.axis_index("grp")
    core, chip, chips = lax.rem(group, 2), group // 2, groups // 2
    partner = {"grp": chip * 2 + 1 - core}
    chip_at = [lax.rem(chip + d, chips) for d in range(chips)]
    dev_at = [lax.rem(me + d, peers) for d in range(peers)]
    greet(
        [partner]
        + [{"grp": chip_at[d] * 2 + core} for d in range(1, chips)]
        + [{"dev": dev_at[d]} for d in range(1, peers)]
    )
    used = [0]

    def make(src, dst, where):
        at = used[0]
        used[0] += 1
        return remote(src, dst, sends.at[at], recvs.at[at], where)

    def run(copies):
        for copy in copies:
            copy.start()
        for copy in copies:
            copy.wait()

    run([make(term.at[1 - core], b1, partner)])
    t1[...] = (term[core].astype(F32) + b1[...].astype(F32)).astype(BF16)
    run([make(t1.at[chip_at[d]], b2.at[d], {"grp": chip_at[d] * 2 + core}) for d in range(1, chips)])
    acc = t1[chip].astype(F32)
    for d in range(1, chips):
        acc = acc + b2[d].astype(F32)
    t2[...] = acc.astype(BF16)
    run([make(t2.at[dev_at[d]], b3.at[d], {"dev": dev_at[d]}) for d in range(1, peers)])
    acc = t2[me].astype(F32)
    for d in range(1, peers):
        acc = acc + b3[d].astype(F32)
    out[core, chip, me] = (acc * scale).astype(BF16)
    mine = out.at[core, chip, me]
    run([make(mine, mine, {"dev": dev_at[d]}) for d in range(1, peers)])
    mine = out.at[core, chip]
    run([make(mine, mine, {"grp": chip_at[d] * 2 + core}) for d in range(1, chips)])
    run([make(out.at[core], out.at[core], partner)])


def params(collective=None):
    more = {} if collective is None else dict(collective_id=collective, has_side_effects=True)
    return pltpu.CompilerParams(vmem_limit_bytes=48 * 1024 * 1024, **more)


def local(queries, query_slots, w_res, labels, blocks, positives):
    peers = lax.axis_size("dev")
    groups = lax.axis_size("grp")
    me = lax.axis_index("dev")
    group = lax.axis_index("grp")
    rows, width = queries.shape
    held = labels.shape[0]
    per = rows // peers
    lines = peers // 2
    chips = groups // 2
    vmem = pl.BlockSpec(memory_space=pltpu.VMEM)
    anywhere = pl.BlockSpec(memory_space=pl.ANY)
    dma = pltpu.SemaphoreType.DMA

    slot_grid = query_slots.reshape(peers, rows)
    slot_sorted = jnp.sort(slot_grid, axis=1)
    own_slots = lax.dynamic_index_in_dim(slot_grid, me, 0, keepdims=False)
    own_sorted = lax.dynamic_index_in_dim(slot_sorted, me, 0, keepdims=False)
    order = (own_sorted[:, None] == own_slots[None, :]).astype(BF16)
    place = lax.dynamic_slice_in_dim(slot_sorted, me * per, per, 1).reshape(rows) - me * rows
    arrange = place[None, :] == jnp.arange(rows, dtype=jnp.int32)[:, None]
    wanted = jnp.sum(jnp.where(arrange[None], positives.T[:, :, None], 0), axis=1)
    meta = jnp.concatenate(
        [wanted, (place // CSIZE)[None], jnp.zeros((8 - NPOS - 1, rows), jnp.int32)], axis=0
    )
    first = (group * peers + me) * held
    listed = blocks.reshape(peers, rows // CSIZE, SHORT) - first
    inside = (listed >= 0) & (listed < held)
    low = jnp.min(jnp.where(inside, listed, held), axis=(1, 2))
    high = jnp.max(jnp.where(inside, listed, -1), axis=(1, 2))
    flag_low = jnp.any(inside & (listed == low[:, None, None]), axis=2).astype(jnp.int32)
    flag_high = jnp.any(inside & (listed == high[:, None, None]), axis=2).astype(jnp.int32)
    flag_high = jnp.where((high > low)[:, None], flag_high, 0)
    table = jnp.concatenate(
        [
            jnp.minimum(low, held - 1)[:, None],
            jnp.maximum(high, 0)[:, None],
            flag_low,
            flag_high,
            jnp.broadcast_to(first * BLK, (peers, 1)),
        ],
        axis=1,
    )

    ordered = jnp.dot(order, queries, preferred_element_type=F32).astype(BF16)
    pre = jnp.dot(ordered, w_res, preferred_element_type=F32)
    hidden = (ordered.astype(F32) + activate(pre)).astype(BF16)

    hall, mall = pl.pallas_call(
        functools.partial(gather_kernel, peers),
        out_shape=(
            jax.ShapeDtypeStruct((peers, peers, per, width), BF16),
            jax.ShapeDtypeStruct((peers, 8, rows), jnp.int32),
        ),
        in_specs=[anywhere, anywhere],
        out_specs=(anywhere, anywhere),
        scratch_shapes=[
            dma((2,)), dma((lines,)), dma((lines,)), dma((lines,)), dma((lines,)),
            dma((lines,)), dma((lines,)), dma((peers,)), dma((peers,)),
        ],
        compiler_params=params(0),
    )(hidden.reshape(peers, per, width), meta)

    grads, losses, label_grad = pl.pallas_call(
        cluster_kernel,
        grid_spec=pltpu.PrefetchScalarGridSpec(
            num_scalar_prefetch=1,
            grid=(peers // 2,),
            in_specs=[
                pl.BlockSpec((peers, 2, per, width), lambda p, t: (0, p, 0, 0)),
                pl.BlockSpec((2, 8, rows), lambda p, t: (p, 0, 0)),
                pl.BlockSpec((held, BLK, width), lambda p, t: (0, 0, 0)),
            ],
            out_specs=[
                pl.BlockSpec((peers, 2, per, width), lambda p, t: (0, p, 0, 0)),
                pl.BlockSpec((2, 8, rows), lambda p, t: (p, 0, 0)),
                pl.BlockSpec((held, BLK, width), lambda p, t: (0, 0, 0)),
            ],
            scratch_shapes=[pltpu.VMEM((held, BLK, width), F32)],
        ),
        out_shape=(
            jax.ShapeDtypeStruct((peers, peers, per, width), BF16),
            jax.ShapeDtypeStruct((peers, 8, rows), F32),
            jax.ShapeDtypeStruct(labels.shape, BF16),
        ),
        compiler_params=params(),
    )(table, hall, mall, labels)

    hidden_grad, loss_sum = pl.pallas_call(
        functools.partial(scatter_kernel, peers),
        out_shape=(
            jax.ShapeDtypeStruct((peers, per, width), BF16),
            jax.ShapeDtypeStruct((8, rows), F32),
        ),
        in_specs=[vmem, vmem],
        out_specs=(vmem, vmem),
        scratch_shapes=[
            pltpu.VMEM((lines, peers, per, width), BF16),
            pltpu.VMEM((lines, peers, per, width), BF16),
            pltpu.VMEM((2, lines, peers, per, width), BF16),
            pltpu.VMEM((peers, per, width), F32),
            pltpu.VMEM((peers, 8, rows), F32),
            dma((lines,)), dma((lines,)), dma((lines,)), dma((2, lines)),
            dma((peers,)), dma((peers,)),
        ],
        compiler_params=params(1),
    )(grads, losses)
    hidden_grad = hidden_grad.reshape(rows, width).astype(F32)

    loss_rows = jnp.sum(jnp.where(arrange, loss_sum[0][None, :], 0.0), axis=1)
    grad_pre = (hidden_grad * activate_slope(pre)).astype(BF16)
    weight_term = lax.dot_general(
        ordered, grad_pre, (((0,), (0,)), ((), ())), preferred_element_type=F32
    )
    tall, wide = width // (2 * chips * lines), width // 2
    pieces = weight_term.astype(BF16).reshape(2, chips, lines, tall, 2, wide)
    pieces = pieces.transpose(0, 1, 4, 2, 3, 5).reshape(2, chips, peers, tall, wide)
    count = 2 + 2 * (chips - 1) + 2 * (peers - 1)
    summed = pl.pallas_call(
        functools.partial(
            sum_kernel, peers, groups, float(rows * peers * groups) ** (-0.5)
        ),
        out_shape=jax.ShapeDtypeStruct(pieces.shape, BF16),
        in_specs=[vmem],
        out_specs=vmem,
        scratch_shapes=[
            pltpu.VMEM((chips, peers, tall, wide), BF16),
            pltpu.VMEM((chips, peers, tall, wide), BF16),
            pltpu.VMEM((chips, peers, tall, wide), BF16),
            pltpu.VMEM((peers, tall, wide), BF16),
            pltpu.VMEM((peers, tall, wide), BF16),
            dma((count,)), dma((count,)),
        ],
        compiler_params=params(2),
    )(pieces)
    residual_grad = summed.reshape(2, chips, 2, lines, tall, wide)
    residual_grad = residual_grad.transpose(0, 1, 3, 4, 2, 5).reshape(width, width)

    back_term = jnp.einsum("qe,de->qd", grad_pre, w_res, preferred_element_type=F32)
    query_grad = (hidden_grad + back_term).astype(BF16)
    query_grad = lax.dot_general(
        order, query_grad, (((0,), (0,)), ((), ())), preferred_element_type=F32
    ).astype(BF16)
    return loss_rows, query_grad, label_grad, residual_grad


def solution(mesh):
    in_specs = (
        P(("grp", "dev"), None),
        P("grp"),
        P(),
        P(("grp", "dev"), None, None),
        P("grp", None),
        P(("grp", "dev"), None),
    )
    out_specs = (P(("grp", "dev")), P(("grp", "dev"), None), P(("grp", "dev"), None, None), P())
    return jax.shard_map(local, mesh=mesh, in_specs=in_specs, out_specs=out_specs, check_vma=False)
```

```python
import functools

import jax
import jax.numpy as jnp
from jax import lax
from jax.experimental import pallas as pl
from jax.experimental.pallas import tpu as pltpu
from jax.sharding import PartitionSpec as P

BLK = 128
CSIZE = 128
SHORT = 12
NPOS = 4
UNITS = 2
MESH = pl.DeviceIdType.MESH
F32 = jnp.float32
BF16 = jnp.bfloat16


def activate(values):
    return jax.nn.gelu(values, approximate=True)


def activate_slope(values):
    return jax.vjp(activate, values)[1](jnp.ones_like(values))[0]


def remote(src, dst, send, recv, where):
    return pltpu.make_async_remote_copy(
        src_ref=src, dst_ref=dst, send_sem=send, recv_sem=recv, device_id=where, device_id_type=MESH
    )


def greet(targets):
    barrier = pltpu.get_barrier_semaphore()
    for where in targets:
        pl.semaphore_signal(barrier, inc=1, device_id=where, device_id_type=MESH)
    pl.semaphore_wait(barrier, len(targets))


def dev_peers(peers):
    me = lax.axis_index("dev")
    return [{"dev": lax.rem(me + d, peers)} for d in range(1, peers)]


def gather_kernel(peers, hid, meta, hall, mall, own, us, ur, ds, dr, ys, yr, ms, mr):
    me = lax.axis_index("dev")
    inner, outer, lines = lax.rem(me, 2), me // 2, peers // 2
    top = lines - 1
    partner = {"dev": outer * 2 + 1 - inner}
    above, below = {"dev": me + 2}, {"dev": me - 2}
    greet(dev_peers(peers))

    def up(k, held=None):
        spot = hall.at[me - 2 * k]
        return remote(spot if held is None else held, spot, us.at[k], ur.at[k], above)

    def down(k, held=None):
        spot = hall.at[me + 2 * k]
        return remote(spot if held is None else held, spot, ds.at[k], dr.at[k], below)

    def across(line, held=None):
        spot = hall.at[line * 2 + inner]
        return remote(spot if held is None else held, spot, ys.at[line], yr.at[line], partner)

    @pl.when(outer < top)
    def _():
        up(0, hid).start()

    @pl.when(outer > 0)
    def _():
        down(0, hid).start()

    across(outer, hid).start()
    local_h = pltpu.make_async_copy(hid, hall.at[me], own.at[0])
    local_m = pltpu.make_async_copy(meta, mall.at[me], own.at[1])
    local_h.start()
    local_m.start()
    small = []
    for d in range(1, peers):
        there = {"dev": lax.rem(me + d, peers)}
        small.append(remote(meta, mall.at[me], ms.at[d], mr.at[d], there))
    for copy in small:
        copy.start()
    for k in range(lines - 1):

        @pl.when(outer >= k + 1)
        def _():
            spot = hall.at[me - 2 * (k + 1)]
            remote(spot, spot, us.at[k], ur.at[k], below).wait_recv()

            @pl.when(outer < top)
            def _():
                up(k + 1).start()

            across(outer - 1 - k).start()

        @pl.when(outer + k + 1 <= top)
        def _():
            spot = hall.at[me + 2 * (k + 1)]
            remote(spot, spot, ds.at[k], dr.at[k], above).wait_recv()

            @pl.when(outer > 0)
            def _():
                down(k + 1).start()

            across(outer + 1 + k).start()

    for k in range(lines):

        @pl.when((outer >= k) & (outer < top))
        def _():
            up(k).wait_send()

        @pl.when((outer + k <= top) & (outer > 0))
        def _():
            down(k).wait_send()

    for line in range(lines):
        across(line).wait()
    for copy in small:
        copy.wait()
    local_h.wait()
    local_m.wait()


def cluster_kernel(table, hall, meta, labels, grads, losses, label_grad, total):
    step = pl.program_id(0)
    peers, owners, per, width = hall.shape
    rows = peers * per

    @pl.when(step == 0)
    def _():
        total[...] = jnp.zeros_like(total)

    lanes = lax.broadcasted_iota(jnp.int32, (BLK, rows), 0)
    for owner in range(owners):
        at = step * owners + owner
        data = hall[:, owner].reshape(rows, width)
        member = meta[owner, NPOS:NPOS + 1, :]
        vectors = jnp.concatenate([labels[table[at, unit]] for unit in range(UNITS)], axis=0)
        logits = lax.dot_general(
            vectors, data, (((1,), (1,)), ((), ())), preferred_element_type=F32
        )
        small = jnp.exp(-jnp.abs(logits))
        soft = jnp.maximum(logits, 0.0) + jnp.log1p(small)
        chance = jnp.where(logits >= 0, 1.0, small) / (1.0 + small)
        loss = jnp.zeros((1, rows), F32)
        parts = []
        for unit in range(UNITS):
            base = table[at, 6] + table[at, unit] * BLK
            listed = jnp.where(member == 0, table[at, 2 + 2 * unit], table[at, 3 + 2 * unit])
            live = listed > 0
            span = slice(unit * BLK, (unit + 1) * BLK)
            hit = lanes == meta[owner, 0:1, :] - base
            for n in range(1, NPOS):
                hit = hit | (lanes == meta[owner, n:n + 1, :] - base)
            gap = soft[span] - jnp.where(hit, logits[span], 0.0)
            loss = loss + jnp.where(live, jnp.sum(gap, axis=0, keepdims=True), 0.0)
            parts.append(jnp.where(live, chance[span] - jnp.where(hit, 1.0, 0.0), 0.0))
        wrong = jnp.concatenate(parts, axis=0).astype(BF16)
        grad = lax.dot_general(
            wrong, vectors, (((0,), (0,)), ((), ())), preferred_element_type=F32
        )
        term = jnp.dot(wrong, data, preferred_element_type=F32).astype(BF16).astype(F32)
        for unit in range(UNITS):
            block = table[at, unit]
            total[block] = total[block] + term[unit * BLK:(unit + 1) * BLK]
        grads[:, owner] = grad.astype(BF16).reshape(peers, per, width)
        losses[owner] = jnp.broadcast_to(loss * (1.0 / (SHORT * BLK)), losses.shape[1:])

    @pl.when(step == pl.num_programs(0) - 1)
    def _():
        label_grad[...] = total[...].astype(BF16)


def scatter_kernel(
    peers, grads, losses, out, loss_out, yb, hb, rb, acc, lb, ys, yr, zs, zr, ls, lr
):
    me = lax.axis_index("dev")
    inner, outer, lines = lax.rem(me, 2), me // 2, peers // 2
    top = lines - 1
    partner = {"dev": outer * 2 + 1 - inner}
    orders = [sorted(range(lines), key=lambda at: -abs(at - o)) for o in range(lines)]
    greet(dev_peers(peers))

    def pick(k):
        line = orders[0][k]
        for o in range(1, lines):
            line = jnp.where(outer == o, orders[o][k], line)
        return line

    picked = [pick(k) for k in range(lines - 1)] + [outer]
    across, along, small = [], [], []
    for k, line in enumerate(picked):
        across.append(remote(grads.at[line * 2 + 1 - inner], yb.at[k], ys.at[k], yr.at[k], partner))
    for d in range(1, peers):
        dest = lax.rem(me + d, peers)
        small.append(remote(losses.at[dest], lb.at[d], ls.at[d], lr.at[d], {"dev": dest}))
    for copy in across + small:
        copy.start()

    def pair(k):
        return grads[picked[k] * 2 + inner].astype(F32) + yb[k].astype(F32)

    for k in range(lines - 1):
        line = picked[k]
        way = jnp.where(line > outer, 0, 1)
        ahead = me + 2 - 4 * way
        feeds = jnp.where(line > outer, outer, top - outer)
        copy = remote(hb.at[k], rb.at[way, line], zs.at[k], zr.at[way, line], {"dev": ahead})
        across[k].wait_recv()

        @pl.when(feeds == 0)
        def _():
            hb[k] = pair(k).astype(BF16)

        @pl.when(feeds > 0)
        def _():
            copy.wait_recv()
            hb[k] = (pair(k) + rb[way, line].astype(F32)).astype(BF16)

        copy.start()
        along.append(copy)
    for copy in small:
        copy.wait()
    loss = losses[me]
    for d in range(1, peers):
        loss = loss + lb[d]
    loss_out[...] = loss
    across[top].wait_recv()
    acc[...] = pair(top)
    for way, present in enumerate((outer > 0, outer < top)):

        @pl.when(present)
        def _():
            spot = rb.at[way, outer]
            near = {"dev": me - 2 + 4 * way}
            remote(spot, spot, zs.at[0], zr.at[way, outer], near).wait_recv()
            acc[...] += rb[way, outer].astype(F32)

    out[...] = acc[...].astype(BF16)
    for copy in across + along:
        copy.wait_send()


def sum_kernel(peers, groups, scale, term, out, b1, t1, own, b2, t2, b3, sends, recvs):
    me, group = lax.axis_index("dev"), lax.axis_index("grp")
    core, chip, chips = lax.rem(group, 2), group // 2, groups // 2
    partner = {"grp": chip * 2 + 1 - core}
    chip_at = [lax.rem(chip + d, chips) for d in range(chips)]
    dev_at = [lax.rem(me + d, peers) for d in range(peers)]
    chip_to = [{"grp": at * 2 + core} for at in chip_at]
    greet([partner] + chip_to[1:] + [{"dev": dev_at[d]} for d in range(1, peers)])
    far, away = range(1, chips), range(1, peers)
    pending = []

    def send(src, dst, where):
        at = len(pending)
        copy = remote(src, dst, sends.at[at], recvs.at[at], where)
        copy.start()
        pending.append(copy)
        return copy

    halves = [
        send(term.at[1 - core, chip_at[d]], b1.at[d], partner) for d in list(far) + [0]
    ]
    across = {}
    for d in far:
        halves[d - 1].wait_recv()
        t1[d] = (term[core, chip_at[d]].astype(F32) + b1[d].astype(F32)).astype(BF16)
        for e in list(away) + [0]:
            across[d, e] = send(t1.at[d, dev_at[e]], b2.at[d, e], chip_to[d])
    halves[-1].wait_recv()
    own[...] = term[core, chip].astype(F32) + b1[0].astype(F32)
    spread = {}
    for e in list(away) + [0]:
        acc = own[dev_at[e]]
        for d in far:
            across[d, e].wait_recv()
            acc = acc + b2[d, e].astype(F32)
        if e > 0:
            t2[e] = acc.astype(BF16)
            spread[e] = send(t2.at[e], b3.at[e], {"dev": dev_at[e]})
    for e in away:
        spread[e].wait_recv()
        acc = acc + b3[e].astype(F32)
    out[core, chip, me] = (acc * scale).astype(BF16)
    mine = out.at[core, chip, me]
    back = {e: send(mine, mine, {"dev": dev_at[e]}) for e in away}
    final = [send(mine, mine, chip_to[d]) for d in far]
    for e in away:
        back[e].wait_recv()
        piece = out.at[core, chip, lax.rem(me + peers - e, peers)]
        final += [send(piece, piece, chip_to[d]) for d in far]
    mine = out.at[core, chip]
    last = [send(mine, mine, partner)]
    for copy in final:
        copy.wait_recv()
    for d in far:
        mine = out.at[core, chip_at[d]]
        last.append(send(mine, mine, partner))
    for copy in last:
        copy.wait_recv()
    for copy in pending:
        copy.wait_send()


def params(collective=None):
    more = {} if collective is None else dict(collective_id=collective, has_side_effects=True)
    return pltpu.CompilerParams(vmem_limit_bytes=48 * 1024 * 1024, **more)


def local(queries, query_slots, w_res, labels, blocks, positives):
    peers = lax.axis_size("dev")
    groups = lax.axis_size("grp")
    me = lax.axis_index("dev")
    group = lax.axis_index("grp")
    rows, width = queries.shape
    held = labels.shape[0]
    per = rows // peers
    lines = peers // 2
    chips = groups // 2
    vmem = pl.BlockSpec(memory_space=pltpu.VMEM)
    anywhere = pl.BlockSpec(memory_space=pl.ANY)
    dma = pltpu.SemaphoreType.DMA

    slot_grid = query_slots.reshape(peers, rows)
    slot_sorted = jnp.sort(slot_grid, axis=1)
    own_slots = lax.dynamic_index_in_dim(slot_grid, me, 0, keepdims=False)
    own_sorted = lax.dynamic_index_in_dim(slot_sorted, me, 0, keepdims=False)
    order = (own_sorted[:, None] == own_slots[None, :]).astype(BF16)
    place = lax.dynamic_slice_in_dim(slot_sorted, me * per, per, 1).reshape(rows) - me * rows
    arrange = place[None, :] == jnp.arange(rows, dtype=jnp.int32)[:, None]
    wanted = jnp.sum(jnp.where(arrange[None], positives.T[:, :, None], 0), axis=1)
    meta = jnp.concatenate(
        [wanted, (place // CSIZE)[None], jnp.zeros((8 - NPOS - 1, rows), jnp.int32)], axis=0
    )
    first = (group * peers + me) * held
    listed = blocks.reshape(peers, rows // CSIZE, SHORT) - first
    inside = (listed >= 0) & (listed < held)
    low = jnp.min(jnp.where(inside, listed, held), axis=(1, 2))
    high = jnp.max(jnp.where(inside, listed, -1), axis=(1, 2))
    flag_low = jnp.any(inside & (listed == low[:, None, None]), axis=2).astype(jnp.int32)
    flag_high = jnp.any(inside & (listed == high[:, None, None]), axis=2).astype(jnp.int32)
    flag_high = jnp.where((high > low)[:, None], flag_high, 0)
    table = jnp.concatenate(
        [
            jnp.minimum(low, held - 1)[:, None],
            jnp.maximum(high, 0)[:, None],
            flag_low,
            flag_high,
            jnp.broadcast_to(first * BLK, (peers, 1)),
        ],
        axis=1,
    )

    ordered = jnp.dot(order, queries, preferred_element_type=F32).astype(BF16)
    pre = jnp.dot(ordered, w_res, preferred_element_type=F32)
    hidden = (ordered.astype(F32) + activate(pre)).astype(BF16)

    hall, mall = pl.pallas_call(
        functools.partial(gather_kernel, peers),
        out_shape=(
            jax.ShapeDtypeStruct((peers, peers, per, width), BF16),
            jax.ShapeDtypeStruct((peers, 8, rows), jnp.int32),
        ),
        in_specs=[anywhere, anywhere],
        out_specs=(anywhere, anywhere),
        scratch_shapes=[
            dma((2,)), dma((lines,)), dma((lines,)), dma((lines,)), dma((lines,)),
            dma((lines,)), dma((lines,)), dma((peers,)), dma((peers,)),
        ],
        compiler_params=params(0),
    )(hidden.reshape(peers, per, width), meta)

    grads, losses, label_grad = pl.pallas_call(
        cluster_kernel,
        grid_spec=pltpu.PrefetchScalarGridSpec(
            num_scalar_prefetch=1,
            grid=(peers // 2,),
            in_specs=[
                pl.BlockSpec((peers, 2, per, width), lambda p, t: (0, p, 0, 0)),
                pl.BlockSpec((2, 8, rows), lambda p, t: (p, 0, 0)),
                pl.BlockSpec((held, BLK, width), lambda p, t: (0, 0, 0)),
            ],
            out_specs=[
                pl.BlockSpec((peers, 2, per, width), lambda p, t: (0, p, 0, 0)),
                pl.BlockSpec((2, 8, rows), lambda p, t: (p, 0, 0)),
                pl.BlockSpec((held, BLK, width), lambda p, t: (0, 0, 0)),
            ],
            scratch_shapes=[pltpu.VMEM((held, BLK, width), F32)],
        ),
        out_shape=(
            jax.ShapeDtypeStruct((peers, peers, per, width), BF16),
            jax.ShapeDtypeStruct((peers, 8, rows), F32),
            jax.ShapeDtypeStruct(labels.shape, BF16),
        ),
        compiler_params=params(),
    )(table, hall, mall, labels)

    hidden_grad, loss_sum = pl.pallas_call(
        functools.partial(scatter_kernel, peers),
        out_shape=(
            jax.ShapeDtypeStruct((peers, per, width), BF16),
            jax.ShapeDtypeStruct((8, rows), F32),
        ),
        in_specs=[vmem, vmem],
        out_specs=(vmem, vmem),
        scratch_shapes=[
            pltpu.VMEM((lines, peers, per, width), BF16),
            pltpu.VMEM((lines, peers, per, width), BF16),
            pltpu.VMEM((2, lines, peers, per, width), BF16),
            pltpu.VMEM((peers, per, width), F32),
            pltpu.VMEM((peers, 8, rows), F32),
            dma((lines,)), dma((lines,)), dma((lines,)), dma((2, lines)),
            dma((peers,)), dma((peers,)),
        ],
        compiler_params=params(1),
    )(grads, losses)
    hidden_grad = hidden_grad.reshape(rows, width).astype(F32)

    loss_rows = jnp.sum(jnp.where(arrange, loss_sum[0][None, :], 0.0), axis=1)
    grad_pre = (hidden_grad * activate_slope(pre)).astype(BF16)
    weight_term = lax.dot_general(
        ordered, grad_pre, (((0,), (0,)), ((), ())), preferred_element_type=F32
    )
    tall, wide = width // (2 * chips * lines), width // 2
    pieces = weight_term.astype(BF16).reshape(2, chips, lines, tall, 2, wide)
    pieces = pieces.transpose(0, 1, 4, 2, 3, 5).reshape(2, chips, peers, tall, wide)
    count = 2 * chips + 2 * (chips - 1) * peers + 2 * (peers - 1)
    summed = pl.pallas_call(
        functools.partial(
            sum_kernel, peers, groups, float(rows * peers * groups) ** (-0.5)
        ),
        out_shape=jax.ShapeDtypeStruct(pieces.shape, BF16),
        in_specs=[vmem],
        out_specs=vmem,
        scratch_shapes=[
            pltpu.VMEM((chips, peers, tall, wide), BF16),
            pltpu.VMEM((chips, peers, tall, wide), BF16),
            pltpu.VMEM((peers, tall, wide), F32),
            pltpu.VMEM((chips, peers, tall, wide), BF16),
            pltpu.VMEM((peers, tall, wide), BF16),
            pltpu.VMEM((peers, tall, wide), BF16),
            dma((count,)), dma((count,)),
        ],
        compiler_params=params(2),
    )(pieces)
    residual_grad = summed.reshape(2, chips, 2, lines, tall, wide)
    residual_grad = residual_grad.transpose(0, 1, 3, 4, 2, 5).reshape(width, width)

    back_term = jnp.einsum("qe,de->qd", grad_pre, w_res, preferred_element_type=F32)
    query_grad = (hidden_grad + back_term).astype(BF16)
    query_grad = lax.dot_general(
        order, query_grad, (((0,), (0,)), ((), ())), preferred_element_type=F32
    ).astype(BF16)
    return loss_rows, query_grad, label_grad, residual_grad


def solution(mesh):
    in_specs = (
        P(("grp", "dev"), None),
        P("grp"),
        P(),
        P(("grp", "dev"), None, None),
        P("grp", None),
        P(("grp", "dev"), None),
    )
    out_specs = (P(("grp", "dev")), P(("grp", "dev"), None), P(("grp", "dev"), None, None), P())
    return jax.shard_map(local, mesh=mesh, in_specs=in_specs, out_specs=out_specs, check_vma=False)
```

```python
import functools

import jax
import jax.numpy as jnp
from jax import lax
from jax.experimental import pallas as pl
from jax.experimental.pallas import tpu as pltpu
from jax.sharding import PartitionSpec as P

BLK = 128
CSIZE = 128
SHORT = 12
NPOS = 4
UNITS = 2
MESH = pl.DeviceIdType.MESH
F32 = jnp.float32
BF16 = jnp.bfloat16


def activate(values):
    return jax.nn.gelu(values, approximate=True)


def activate_slope(values):
    return jax.vjp(activate, values)[1](jnp.ones_like(values))[0]


def remote(src, dst, send, recv, where):
    return pltpu.make_async_remote_copy(
        src_ref=src, dst_ref=dst, send_sem=send, recv_sem=recv, device_id=where, device_id_type=MESH
    )


def greet(targets):
    barrier = pltpu.get_barrier_semaphore()
    for where in targets:
        pl.semaphore_signal(barrier, inc=1, device_id=where, device_id_type=MESH)
    pl.semaphore_wait(barrier, len(targets))


def dev_peers(peers):
    me = lax.axis_index("dev")
    return [{"dev": lax.rem(me + d, peers)} for d in range(1, peers)]


def gather_kernel(peers, hid, meta, hall, mall, own, us, ur, ds, dr, ys, yr, ms, mr):
    me = lax.axis_index("dev")
    inner, outer, lines = lax.rem(me, 2), me // 2, peers // 2
    top = lines - 1
    partner = {"dev": outer * 2 + 1 - inner}
    above, below = {"dev": me + 2}, {"dev": me - 2}
    greet(dev_peers(peers))

    def up(k, held=None):
        spot = hall.at[me - 2 * k]
        return remote(spot if held is None else held, spot, us.at[k], ur.at[k], above)

    def down(k, held=None):
        spot = hall.at[me + 2 * k]
        return remote(spot if held is None else held, spot, ds.at[k], dr.at[k], below)

    def across(line, held=None):
        spot = hall.at[line * 2 + inner]
        return remote(spot if held is None else held, spot, ys.at[line], yr.at[line], partner)

    @pl.when(outer < top)
    def _():
        up(0, hid).start()

    @pl.when(outer > 0)
    def _():
        down(0, hid).start()

    across(outer, hid).start()
    local_h = pltpu.make_async_copy(hid, hall.at[me], own.at[0])
    local_m = pltpu.make_async_copy(meta, mall.at[me], own.at[1])
    local_h.start()
    local_m.start()
    small = []
    for d in range(1, peers):
        there = {"dev": lax.rem(me + d, peers)}
        small.append(remote(meta, mall.at[me], ms.at[d], mr.at[d], there))
    for copy in small:
        copy.start()
    for k in range(lines - 1):

        @pl.when(outer >= k + 1)
        def _():
            spot = hall.at[me - 2 * (k + 1)]
            remote(spot, spot, us.at[k], ur.at[k], below).wait_recv()

            @pl.when(outer < top)
            def _():
                up(k + 1).start()

            across(outer - 1 - k).start()

        @pl.when(outer + k + 1 <= top)
        def _():
            spot = hall.at[me + 2 * (k + 1)]
            remote(spot, spot, ds.at[k], dr.at[k], above).wait_recv()

            @pl.when(outer > 0)
            def _():
                down(k + 1).start()

            across(outer + 1 + k).start()

    for k in range(lines):

        @pl.when((outer >= k) & (outer < top))
        def _():
            up(k).wait_send()

        @pl.when((outer + k <= top) & (outer > 0))
        def _():
            down(k).wait_send()

    for line in range(lines):
        across(line).wait()
    for copy in small:
        copy.wait()
    local_h.wait()
    local_m.wait()


def cluster_kernel(table, hall, meta, labels, grads, losses, label_grad, total):
    step = pl.program_id(0)
    peers, owners, per, width = hall.shape
    rows = peers * per

    @pl.when(step == 0)
    def _():
        total[...] = jnp.zeros_like(total)

    lanes = lax.broadcasted_iota(jnp.int32, (BLK, rows), 0)
    for owner in range(owners):
        at = step * owners + owner
        data = hall[:, owner].reshape(rows, width)
        member = meta[owner, NPOS:NPOS + 1, :]
        vectors = jnp.concatenate([labels[table[at, unit]] for unit in range(UNITS)], axis=0)
        logits = lax.dot_general(
            vectors, data, (((1,), (1,)), ((), ())), preferred_element_type=F32
        )
        small = jnp.exp(-jnp.abs(logits))
        soft = jnp.maximum(logits, 0.0) + jnp.log1p(small)
        chance = jnp.where(logits >= 0, 1.0, small) / (1.0 + small)
        loss = jnp.zeros((1, rows), F32)
        parts = []
        for unit in range(UNITS):
            base = table[at, 6] + table[at, unit] * BLK
            listed = jnp.where(member == 0, table[at, 2 + 2 * unit], table[at, 3 + 2 * unit])
            live = listed > 0
            span = slice(unit * BLK, (unit + 1) * BLK)
            hit = lanes == meta[owner, 0:1, :] - base
            for n in range(1, NPOS):
                hit = hit | (lanes == meta[owner, n:n + 1, :] - base)
            gap = soft[span] - jnp.where(hit, logits[span], 0.0)
            loss = loss + jnp.where(live, jnp.sum(gap, axis=0, keepdims=True), 0.0)
            parts.append(jnp.where(live, chance[span] - jnp.where(hit, 1.0, 0.0), 0.0))
        wrong = jnp.concatenate(parts, axis=0).astype(BF16)
        grad = lax.dot_general(
            wrong, vectors, (((0,), (0,)), ((), ())), preferred_element_type=F32
        )
        term = jnp.dot(wrong, data, preferred_element_type=F32).astype(BF16).astype(F32)
        for unit in range(UNITS):
            block = table[at, unit]
            total[block] = total[block] + term[unit * BLK:(unit + 1) * BLK]
        grads[:, owner] = grad.astype(BF16).reshape(peers, per, width)
        losses[owner] = jnp.broadcast_to(loss * (1.0 / (SHORT * BLK)), losses.shape[1:])

    @pl.when(step == pl.num_programs(0) - 1)
    def _():
        label_grad[...] = total[...].astype(BF16)


def scatter_kernel(
    peers, grads, losses, out, loss_out, yb, hb, rb, acc, lb, ys, yr, zs, zr, ls, lr
):
    me = lax.axis_index("dev")
    inner, outer, lines = lax.rem(me, 2), me // 2, peers // 2
    top = lines - 1
    partner = {"dev": outer * 2 + 1 - inner}
    orders = [sorted(range(lines), key=lambda at: -abs(at - o)) for o in range(lines)]
    greet(dev_peers(peers))

    def pick(k):
        line = orders[0][k]
        for o in range(1, lines):
            line = jnp.where(outer == o, orders[o][k], line)
        return line

    picked = [pick(k) for k in range(lines - 1)] + [outer]
    across, along, small = [], [], []
    for k, line in enumerate(picked):
        across.append(remote(grads.at[line * 2 + 1 - inner], yb.at[k], ys.at[k], yr.at[k], partner))
    for d in range(1, peers):
        dest = lax.rem(me + d, peers)
        small.append(remote(losses.at[dest], lb.at[d], ls.at[d], lr.at[d], {"dev": dest}))
    for copy in across + small:
        copy.start()

    def pair(k):
        return grads[picked[k] * 2 + inner].astype(F32) + yb[k].astype(F32)

    for k in range(lines - 1):
        line = picked[k]
        way = jnp.where(line > outer, 0, 1)
        ahead = me + 2 - 4 * way
        feeds = jnp.where(line > outer, outer, top - outer)
        copy = remote(hb.at[k], rb.at[way, line], zs.at[k], zr.at[way, line], {"dev": ahead})
        across[k].wait_recv()

        @pl.when(feeds == 0)
        def _():
            hb[k] = pair(k).astype(BF16)

        @pl.when(feeds > 0)
        def _():
            copy.wait_recv()
            hb[k] = (pair(k) + rb[way, line].astype(F32)).astype(BF16)

        copy.start()
        along.append(copy)
    for copy in small:
        copy.wait()
    loss = losses[me]
    for d in range(1, peers):
        loss = loss + lb[d]
    loss_out[...] = loss
    across[top].wait_recv()
    acc[...] = pair(top)
    for way, present in enumerate((outer > 0, outer < top)):

        @pl.when(present)
        def _():
            spot = rb.at[way, outer]
            near = {"dev": me - 2 + 4 * way}
            remote(spot, spot, zs.at[0], zr.at[way, outer], near).wait_recv()
            acc[...] += rb[way, outer].astype(F32)

    out[...] = acc[...].astype(BF16)
    for copy in across + along:
        copy.wait_send()


def sum_kernel(peers, groups, scale, term, out, b1, t1, own, b2, t2, b3, sends, recvs):
    me, group = lax.axis_index("dev"), lax.axis_index("grp")
    core, chip, chips = lax.rem(group, 2), group // 2, groups // 2
    partner = {"grp": chip * 2 + 1 - core}
    chip_at = [lax.rem(chip + d, chips) for d in range(chips)]
    dev_at = [lax.rem(me + d, peers) for d in range(peers)]
    chip_to = [{"grp": at * 2 + core} for at in chip_at]
    greet([partner] + chip_to[1:] + [{"dev": dev_at[d]} for d in range(1, peers)])
    far, away = range(1, chips), range(1, peers)
    pending = []

    def send(src, dst, where):
        at = len(pending)
        copy = remote(src, dst, sends.at[at], recvs.at[at], where)
        copy.start()
        pending.append(copy)
        return copy

    halves = [
        send(term.at[1 - core, chip_at[d]], b1.at[d], partner) for d in list(far) + [0]
    ]
    across = {}
    for d in far:
        halves[d - 1].wait_recv()
        t1[d] = (term[core, chip_at[d]].astype(F32) + b1[d].astype(F32)).astype(BF16)
        for e in list(away) + [0]:
            across[d, e] = send(t1.at[d, dev_at[e]], b2.at[d, e], chip_to[d])
    halves[-1].wait_recv()
    own[...] = term[core, chip].astype(F32) + b1[0].astype(F32)
    spread = {}
    for e in list(away) + [0]:
        acc = own[dev_at[e]]
        for d in far:
            across[d, e].wait_recv()
            acc = acc + b2[d, e].astype(F32)
        if e > 0:
            t2[e] = acc.astype(BF16)
            spread[e] = send(t2.at[e], b3.at[e], {"dev": dev_at[e]})
    for e in away:
        spread[e].wait_recv()
        acc = acc + b3[e].astype(F32)
    out[core, chip, me] = (acc * scale).astype(BF16)
    mine = out.at[core, chip, me]
    back = {e: send(mine, mine, {"dev": dev_at[e]}) for e in away}
    final = [send(mine, mine, chip_to[d]) for d in far]
    for e in away:
        back[e].wait_recv()
        piece = out.at[core, chip, lax.rem(me + peers - e, peers)]
        final += [send(piece, piece, chip_to[d]) for d in far]
    mine = out.at[core, chip]
    last = [send(mine, mine, partner)]
    for copy in final:
        copy.wait_recv()
    for d in far:
        mine = out.at[core, chip_at[d]]
        last.append(send(mine, mine, partner))
    for copy in last:
        copy.wait_recv()
    for copy in pending:
        copy.wait_send()


def params(collective=None, limit=48):
    more = {} if collective is None else dict(collective_id=collective, has_side_effects=True)
    return pltpu.CompilerParams(vmem_limit_bytes=limit * 1024 * 1024, **more)


def local(queries, query_slots, w_res, labels, blocks, positives):
    peers = lax.axis_size("dev")
    groups = lax.axis_size("grp")
    me = lax.axis_index("dev")
    group = lax.axis_index("grp")
    rows, width = queries.shape
    held = labels.shape[0]
    per = rows // peers
    lines = peers // 2
    chips = groups // 2
    vmem = pl.BlockSpec(memory_space=pltpu.VMEM)
    anywhere = pl.BlockSpec(memory_space=pl.ANY)
    dma = pltpu.SemaphoreType.DMA

    slot_grid = query_slots.reshape(peers, rows)
    slot_sorted = jnp.sort(slot_grid, axis=1)
    own_slots = lax.dynamic_index_in_dim(slot_grid, me, 0, keepdims=False)
    own_sorted = lax.dynamic_index_in_dim(slot_sorted, me, 0, keepdims=False)
    order = (own_sorted[:, None] == own_slots[None, :]).astype(BF16)
    place = lax.dynamic_slice_in_dim(slot_sorted, me * per, per, 1).reshape(rows) - me * rows
    arrange = place[None, :] == jnp.arange(rows, dtype=jnp.int32)[:, None]
    wanted = jnp.sum(jnp.where(arrange[None], positives.T[:, :, None], 0), axis=1)
    meta = jnp.concatenate(
        [wanted, (place // CSIZE)[None], jnp.zeros((8 - NPOS - 1, rows), jnp.int32)], axis=0
    )
    first = (group * peers + me) * held
    listed = blocks.reshape(peers, rows // CSIZE, SHORT) - first
    inside = (listed >= 0) & (listed < held)
    low = jnp.min(jnp.where(inside, listed, held), axis=(1, 2))
    high = jnp.max(jnp.where(inside, listed, -1), axis=(1, 2))
    flag_low = jnp.any(inside & (listed == low[:, None, None]), axis=2).astype(jnp.int32)
    flag_high = jnp.any(inside & (listed == high[:, None, None]), axis=2).astype(jnp.int32)
    flag_high = jnp.where((high > low)[:, None], flag_high, 0)
    table = jnp.concatenate(
        [
            jnp.minimum(low, held - 1)[:, None],
            jnp.maximum(high, 0)[:, None],
            flag_low,
            flag_high,
            jnp.broadcast_to(first * BLK, (peers, 1)),
        ],
        axis=1,
    )

    ordered = jnp.dot(order, queries, preferred_element_type=F32).astype(BF16)
    pre = jnp.dot(ordered, w_res, preferred_element_type=F32)
    hidden = (ordered.astype(F32) + activate(pre)).astype(BF16)

    hall, mall = pl.pallas_call(
        functools.partial(gather_kernel, peers),
        out_shape=(
            jax.ShapeDtypeStruct((peers, peers, per, width), BF16),
            jax.ShapeDtypeStruct((peers, 8, rows), jnp.int32),
        ),
        in_specs=[anywhere, anywhere],
        out_specs=(anywhere, anywhere),
        scratch_shapes=[
            dma((2,)), dma((lines,)), dma((lines,)), dma((lines,)), dma((lines,)),
            dma((lines,)), dma((lines,)), dma((peers,)), dma((peers,)),
        ],
        compiler_params=params(0, 62),
    )(hidden.reshape(peers, per, width), meta)

    grads, losses, label_grad = pl.pallas_call(
        cluster_kernel,
        grid_spec=pltpu.PrefetchScalarGridSpec(
            num_scalar_prefetch=1,
            grid=(peers // 2,),
            in_specs=[
                pl.BlockSpec((peers, 2, per, width), lambda p, t: (0, p, 0, 0)),
                pl.BlockSpec((2, 8, rows), lambda p, t: (p, 0, 0)),
                pl.BlockSpec((held, BLK, width), lambda p, t: (0, 0, 0)),
            ],
            out_specs=[
                pl.BlockSpec((peers, 2, per, width), lambda p, t: (0, p, 0, 0)),
                pl.BlockSpec((2, 8, rows), lambda p, t: (p, 0, 0)),
                pl.BlockSpec((held, BLK, width), lambda p, t: (0, 0, 0)),
            ],
            scratch_shapes=[pltpu.VMEM((held, BLK, width), F32)],
        ),
        out_shape=(
            jax.ShapeDtypeStruct((peers, peers, per, width), BF16),
            jax.ShapeDtypeStruct((peers, 8, rows), F32),
            jax.ShapeDtypeStruct(labels.shape, BF16),
        ),
        compiler_params=params(limit=62),
    )(table, hall, mall, labels)

    hidden_grad, loss_sum = pl.pallas_call(
        functools.partial(scatter_kernel, peers),
        out_shape=(
            jax.ShapeDtypeStruct((peers, per, width), BF16),
            jax.ShapeDtypeStruct((8, rows), F32),
        ),
        in_specs=[vmem, vmem],
        out_specs=(vmem, vmem),
        scratch_shapes=[
            pltpu.VMEM((lines, peers, per, width), BF16),
            pltpu.VMEM((lines, peers, per, width), BF16),
            pltpu.VMEM((2, lines, peers, per, width), BF16),
            pltpu.VMEM((peers, per, width), F32),
            pltpu.VMEM((peers, 8, rows), F32),
            dma((lines,)), dma((lines,)), dma((lines,)), dma((2, lines)),
            dma((peers,)), dma((peers,)),
        ],
        compiler_params=params(1),
    )(grads, losses)
    hidden_grad = hidden_grad.reshape(rows, width).astype(F32)

    loss_rows = jnp.sum(jnp.where(arrange, loss_sum[0][None, :], 0.0), axis=1)
    grad_pre = (hidden_grad * activate_slope(pre)).astype(BF16)
    weight_term = lax.dot_general(
        ordered, grad_pre, (((0,), (0,)), ((), ())), preferred_element_type=F32
    )
    tall, wide = width // (2 * chips * lines), width // 2
    pieces = weight_term.astype(BF16).reshape(2, chips, lines, tall, 2, wide)
    pieces = pieces.transpose(0, 1, 4, 2, 3, 5).reshape(2, chips, peers, tall, wide)
    count = 2 * chips + 2 * (chips - 1) * peers + 2 * (peers - 1)
    summed = pl.pallas_call(
        functools.partial(
            sum_kernel, peers, groups, float(rows * peers * groups) ** (-0.5)
        ),
        out_shape=jax.ShapeDtypeStruct(pieces.shape, BF16),
        in_specs=[vmem],
        out_specs=vmem,
        scratch_shapes=[
            pltpu.VMEM((chips, peers, tall, wide), BF16),
            pltpu.VMEM((chips, peers, tall, wide), BF16),
            pltpu.VMEM((peers, tall, wide), F32),
            pltpu.VMEM((chips, peers, tall, wide), BF16),
            pltpu.VMEM((peers, tall, wide), BF16),
            pltpu.VMEM((peers, tall, wide), BF16),
            dma((count,)), dma((count,)),
        ],
        compiler_params=params(2),
    )(pieces)
    residual_grad = summed.reshape(2, chips, 2, lines, tall, wide)
    residual_grad = residual_grad.transpose(0, 1, 3, 4, 2, 5).reshape(width, width)

    back_term = jnp.einsum("qe,de->qd", grad_pre, w_res, preferred_element_type=F32)
    query_grad = (hidden_grad + back_term).astype(BF16)
    query_grad = lax.dot_general(
        order, query_grad, (((0,), (0,)), ((), ())), preferred_element_type=F32
    ).astype(BF16)
    return loss_rows, query_grad, label_grad, residual_grad


def solution(mesh):
    in_specs = (
        P(("grp", "dev"), None),
        P("grp"),
        P(),
        P(("grp", "dev"), None, None),
        P("grp", None),
        P(("grp", "dev"), None),
    )
    out_specs = (P(("grp", "dev")), P(("grp", "dev"), None), P(("grp", "dev"), None, None), P())
    return jax.shard_map(local, mesh=mesh, in_specs=in_specs, out_specs=out_specs, check_vma=False)
```
